32 devices in a mesh: row: 4 (over y, x), col: 8 (over z, core).
Axes of the slice: x: 2, y: 2, z: 4, core: 2. Of those that a mesh axis runs over, the one named last changes fastest.
Arguments:
- adjacency: bfloat16 [8192, 8192], P('row', 'col'), as said below
- tile_mask: int32 [64, 64], P('row', 'col'), may hold values from 0 to 1, as said below
- out_grad: bfloat16 [8192, 256], P(('row', 'col')), may hold values from -6 to 6
- pre_two: bfloat16 [8192, 256], P(('row', 'col')), may hold values from -6 to 6
- hidden: bfloat16 [8192, 256], P(('col', 'row')), may hold values from -6 to 6
- pre_one: bfloat16 [8192, 256], P(('col', 'row')), may hold values from -6 to 6
- features: bfloat16 [8192, 256], P(('row', 'col')), may hold values from -6 to 6
- w_two: bfloat16 [256, 256], replicated, may hold values from -0.375 to 0.375
- w_one: bfloat16 [256, 256], replicated, may hold values from -0.375 to 0.375
Outputs:
- node_grad: bfloat16 [8192, 256], P(('row', 'col'))
- weight_grad_one: float32 [256, 256], replicated
- weight_grad_two: float32 [256, 256], replicated
The draws below stay inside these ranges and needn't reach their ends.
Inputs may be any that keep to these rules, and one draw needn't show every extreme that they name: adjacency is symmetric and nonnegative. tile_mask is symmetric and every diagonal tile is 1.
All inputs are finite; a program needn't handle non-finite values.
Results may differ from the reference program's by a relative error of at most 0.02.
Values may be sent and summed in bfloat16 or wider, within the bound.
No kernel may reach another device: no remote copies, remote signals or barrier semaphores. Data moves between devices by JAX's collectives and lax.ppermute only.
A program may use at most 128 MiB of HBM per device.

```python
import math
import jax
import jax.numpy as jnp
from jax import lax

F = 256
TILE = 128
NODE_DEV = 256
NODES = 8192
N_ROW = 4
N_COL = 8


def draw_adjacency(key, part):
    levels = jax.random.randint(key, (NODES, NODES), 0, 20480)
    kept_scale = 2.0 / math.sqrt(0.05 * NODES)
    values = (0.5 + levels.astype(jnp.float32) * (1.0 / 1024.0)) * kept_scale
    upper = jnp.where(levels < 1024, values, jnp.zeros_like(values))
    row_ids = lax.broadcasted_iota(jnp.int32, (NODES, 1), 0)
    col_ids = lax.broadcasted_iota(jnp.int32, (1, NODES), 1)
    symmetric = jnp.where(row_ids <= col_ids, upper, upper.T)
    return symmetric.astype(jnp.bfloat16)


def draw_tile_mask(key, part):
    tile_count = NODES // TILE
    group_count = 8
    levels = jax.random.randint(jax.random.fold_in(key, 1), (group_count,), 1, 9)
    group_ids = lax.broadcasted_iota(jnp.int32, (tile_count,), 0) * group_count // tile_count
    group_onehot = (group_ids[:, None] == jnp.arange(group_count, dtype=jnp.int32)[None, :]).astype(jnp.int32)
    tile_level = jnp.sum(group_onehot * levels[None, :], axis=1)
    odds = tile_level[:, None] * tile_level[None, :]
    tosses = jax.random.randint(jax.random.fold_in(key, 2), (tile_count, tile_count), 0, 64)
    hits = (tosses < odds).astype(jnp.int32)
    row_ids = lax.broadcasted_iota(jnp.int32, (tile_count, 1), 0)
    col_ids = lax.broadcasted_iota(jnp.int32, (1, tile_count), 1)
    symmetric = jnp.where(row_ids <= col_ids, hits, hits.T)
    return jnp.where(row_ids == col_ids, jnp.ones_like(symmetric), symmetric).astype(jnp.int32)


def strengthened(drawn, key, source, target, blocks, factor):
    owner, partner = [(jnp.arange(drawn.shape[position]) // (drawn.shape[position] // blocks)).reshape([-1 if axis == position else 1 for axis in range(drawn.ndim)]) for position in (source, target)]
    chosen = jax.random.permutation(key, blocks)[partner]
    strong = (owner == chosen) | (owner == (partner + blocks // 2) % blocks)
    return jnp.where(strong, factor * drawn, drawn)


def steps_of(key, dims, split, low, high):
    gain = 1.0
    for dim, blocks in split:
        heights = jax.random.uniform(jax.random.fold_in(jax.random.fold_in(key, 6), dim), (blocks,), jnp.float32, low / len(split), high / len(split))
        gain = gain * jnp.repeat(jnp.exp(heights), dims[dim] // blocks).reshape((-1,) + (1,) * (len(dims) - 1 - dim))
    return gain


def scatter_about(rng, extent, scale, most, cuts=(), held_as=jnp.bfloat16):
    result = jax.random.normal(rng, extent, jnp.float32) * scale
    if len(cuts) > 0:
        result = steps_of(rng, extent, cuts, -0.22, 0.18) * result
    return jnp.clip(result, min=-most, max=most).astype(held_as)


def heavy_noise(key, extent, deviation, most, cuts, heavy, held_as=jnp.bfloat16):
    array = deviation * jax.random.normal(key, extent, jnp.float32)
    if cuts:
        array = array * steps_of(key, extent, cuts, -0.22, 0.18)
    return jnp.clip(strengthened(array, jax.random.fold_in(key, 3), *heavy), -most, most).astype(held_as)


def setup_inputs(seed: int = 0) -> dict:
    seeds = jax.random.split(jax.random.key(seed), 10)
    return {
        "adjacency": draw_adjacency(jax.random.fold_in(seeds[9], 71), 0),
        "tile_mask": draw_tile_mask(jax.random.fold_in(seeds[9], 71), 0),
        "out_grad": scatter_about(seeds[2], (NODES, F), 1.0, 6.0, ((0, 32),)),
        "pre_two": scatter_about(seeds[3], (NODES, F), 1.0, 6.0, ((0, 32),)),
        "hidden": heavy_noise(seeds[4], (NODES, F), 1.0, 6.0, ((0, 32),), (0, 1, 32, 2.75)),
        "pre_one": scatter_about(seeds[5], (NODES, F), 1.0, 6.0, ((0, 32),)),
        "features": scatter_about(seeds[6], (NODES, F), 1.0, 6.0, ((0, 32),)),
        "w_two": scatter_about(seeds[7], (F, F), F ** -0.5, 0.375),
        "w_one": scatter_about(seeds[8], (F, F), F ** -0.5, 0.375),
    }


def propagate(adjacency, tile_mask, gradient, groups):
    node_count = adjacency.shape[0]
    tile_size = node_count // tile_mask.shape[0]
    block_rows = math.gcd(node_count, 2048)
    width = gradient.shape[1]
    group_nodes = node_count // groups
    dense_grad = gradient.astype(jnp.float32).reshape(groups, group_nodes, width)

    def block_product(block_index):
        graph_rows = lax.dynamic_slice_in_dim(adjacency, block_index * block_rows, block_rows, 0)
        mask_rows = lax.dynamic_slice_in_dim(tile_mask, block_index * (block_rows // tile_size), block_rows // tile_size, 0)
        mask_full = jnp.repeat(jnp.repeat(mask_rows.astype(jnp.float32), tile_size, 0), tile_size, 1)
        weighted = (graph_rows.astype(jnp.float32) * mask_full).reshape(block_rows, groups, group_nodes)
        partial_terms = jnp.einsum("bgk,gkf->gbf", weighted, dense_grad, precision=lax.Precision.HIGHEST)
        rounded = lax.optimization_barrier(partial_terms.astype(jnp.bfloat16))
        return jnp.sum(rounded.astype(jnp.float32), axis=0)

    indices = jnp.arange(node_count // block_rows).astype(jnp.int32)
    return lax.map(block_product, indices).reshape(node_count, width)


def reference(adjacency, tile_mask, out_grad, pre_two, hidden, pre_one, features, w_two, w_one):
    weight_scale = 4.0 * NODE_DEV ** -0.5
    grad_two = jnp.where(pre_two > 0, out_grad, jnp.zeros_like(out_grad))
    prop_two = propagate(adjacency, tile_mask, grad_two, N_ROW).astype(jnp.bfloat16)
    weight_grad_two = jnp.dot(hidden.T, prop_two, preferred_element_type=jnp.float32) * weight_scale
    back_grad = jnp.dot(prop_two, w_two.T, preferred_element_type=jnp.float32)
    grad_one = jnp.where(pre_one > 0, back_grad, jnp.zeros_like(back_grad)).astype(jnp.bfloat16)
    prop_one = propagate(adjacency, tile_mask, grad_one, N_COL).astype(jnp.bfloat16)
    weight_grad_one = jnp.dot(features.T, prop_one, preferred_element_type=jnp.float32) * weight_scale
    node_grad = jnp.dot(prop_one, w_one.T, preferred_element_type=jnp.float32).astype(jnp.bfloat16)
    return node_grad, weight_grad_one, weight_grad_two
```

```python
import functools

import jax
import jax.numpy as jnp
from jax import lax
from jax.experimental import pallas as pl
from jax.experimental.pallas import tpu as pltpu
from jax.sharding import PartitionSpec as P

BF16, F32 = jnp.bfloat16, jnp.float32
ROWS_COLS = (((0,), (0,)), ((), ()))
LAST_LAST = (((1,), (1,)), ((), ()))
VMEM = pltpu.VMEM


def params():
    return pltpu.CompilerParams(vmem_limit_bytes=40 * 1024 * 1024)


def cost(flops, bytes_accessed):
    return pl.CostEstimate(flops=flops, bytes_accessed=bytes_accessed, transcendentals=0)


def whole(count):
    return [pl.BlockSpec(memory_space=VMEM) for _ in range(count)]


def tree(values):
    while len(values) > 1:
        values = [a + b for a, b in zip(values[::2], values[1::2])]
    return values[0]


def mask_kernel(block, tile, row_src, col_src, mask, adj, plain, turned):
    step = pl.program_id(0)
    per = block // tile
    row = row_src[step]
    for slot in range(adj.shape[1] // block):
        col = col_src[slot]
        for v in range(per):
            part = adj[:, pl.ds(pl.multiple_of((col * per + v) * tile, tile), tile)]
            for u in range(per):
                keep = mask[row * per + u, col * per + v].astype(F32).astype(BF16)
                kept = part[u * tile : (u + 1) * tile] * keep
                lanes = slice(slot * block + v * tile, slot * block + (v + 1) * tile)
                plain[u * tile : (u + 1) * tile, lanes] = kept
                turned[lanes, u * tile : (u + 1) * tile] = kept.T


def masked(adjacency, tile_mask, row_src, col_src, block):
    rows, cols = adjacency.shape
    tile = rows // tile_mask.shape[0]
    return pl.pallas_call(
        functools.partial(mask_kernel, block, tile),
        grid_spec=pltpu.PrefetchScalarGridSpec(
            num_scalar_prefetch=3,
            grid=(rows // block,),
            in_specs=[pl.BlockSpec((block, cols), lambda s, row_src, *_: (row_src[s], 0))],
            out_specs=[
                pl.BlockSpec((block, cols), lambda s, *_: (s, 0)),
                pl.BlockSpec((cols, block), lambda s, *_: (0, s)),
            ],
        ),
        out_shape=[
            jax.ShapeDtypeStruct((rows, cols), BF16),
            jax.ShapeDtypeStruct((cols, rows), BF16),
        ],
        compiler_params=params(),
        cost_estimate=cost(rows * cols, 6 * rows * cols),
        name="mask_tiles",
    )(row_src, col_src, tile_mask, adjacency)


def spread_kernel(count, turned, *refs):
    parts, out, held = refs[:count], refs[count], refs[count + 1]
    block = parts[0].shape[0]

    @pl.when(pl.program_id(0) == 0)
    def _():
        for slot, part in enumerate(parts):
            held[slot * block : (slot + 1) * block] = part[...]

    out[0] = jnp.dot(turned[...], held[...], preferred_element_type=F32).astype(BF16)


def spread(graph, parts):
    block, width = parts[0].shape
    rows, cols = graph.shape
    return pl.pallas_call(
        functools.partial(spread_kernel, len(parts)),
        grid=(rows // block,),
        in_specs=[pl.BlockSpec((block, cols), lambda s: (s, 0))]
        + [pl.BlockSpec((block, width), lambda s: (0, 0)) for _ in parts],
        out_specs=pl.BlockSpec((1, block, width), lambda s: (s, 0, 0)),
        out_shape=jax.ShapeDtypeStruct((rows // block, block, width), BF16),
        scratch_shapes=[VMEM((cols, width), BF16)],
        compiler_params=params(),
        cost_estimate=cost(2 * rows * cols * width, 2 * rows * cols),
        name="propagate",
    )(graph, *parts)


def middle_kernel(count, *refs):
    parts, w_two, pre_one = refs[:count], refs[count], refs[count + 1]
    prop, grad = refs[count + 2 :]
    total = tree([part[...].astype(F32) for part in parts]).astype(BF16)
    prop[...] = total
    back = lax.dot_general(total, w_two[...], LAST_LAST, preferred_element_type=F32)
    grad[...] = jnp.where(pre_one[...] > 0, back, 0.0).astype(BF16)


def middle(parts, w_two, pre_one):
    shape = jax.ShapeDtypeStruct(pre_one.shape, BF16)
    return pl.pallas_call(
        functools.partial(middle_kernel, len(parts)),
        in_specs=whole(len(parts) + 2),
        out_specs=whole(2),
        out_shape=[shape, shape],
        compiler_params=params(),
        name="first_layer_gradient",
    )(*parts, w_two, pre_one)


def last_kernel(count, *refs):
    parts, w_one, out = refs[:count], refs[count], refs[count + 1]
    total = tree([part[...].astype(F32) for part in parts]).astype(BF16)
    out[...] = lax.dot_general(
        total, w_one[...], LAST_LAST, preferred_element_type=F32
    ).astype(BF16)


def last(parts, w_one):
    return pl.pallas_call(
        functools.partial(last_kernel, len(parts)),
        in_specs=whole(len(parts) + 1),
        out_specs=pl.BlockSpec(memory_space=VMEM),
        out_shape=jax.ShapeDtypeStruct(parts[0].shape, BF16),
        compiler_params=params(),
        name="node_gradient",
    )(*parts, w_one)


def local(n_row, n_col, adjacency, tile_mask, out_grad, pre_two, hidden, pre_one, features, w_two, w_one):
    block = out_grad.shape[0]
    scale = 4.0 * block ** (-0.5)
    n_far = n_col // 2
    row, col = lax.axis_index("row"), lax.axis_index("col")

    def over_col(value, flip):
        return lax.ppermute(value, "col", [(i, i ^ flip) for i in range(n_col)])

    def over_row(value, flip):
        return lax.ppermute(value, "row", [(i, i ^ flip) for i in range(n_row)])

    def far(value):
        return [value] + [over_col(value, 2 * j) for j in range(1, n_far)]

    def rows_all(value):
        return [value] + [over_row(value, i) for i in range(1, n_row)]

    row_src = jnp.bitwise_xor(jnp.arange(n_col, dtype=jnp.int32), col)
    col_src = jnp.bitwise_xor(jnp.arange(n_row, dtype=jnp.int32), row)

    grad_two = jnp.where(pre_two > 0, out_grad, jnp.zeros_like(out_grad))
    near = far(grad_two)
    plain, turned = masked(adjacency, tile_mask, row_src, col_src, block)
    others = [over_col(value, 1) for value in near]
    second = [value for pair in zip(near, others) for value in pair]
    column_part = spread(turned, second)
    parts = [column_part[0]] + [over_row(column_part[i], i) for i in range(1, n_row)]
    prop_two, grad_one = middle(parts, w_two, pre_one)
    first = rows_all(grad_one)

    near_features = far(features)
    other_features = [over_col(value, 1) for value in near_features]
    term_two = lax.dot_general(hidden, prop_two, ROWS_COLS, preferred_element_type=F32)

    row_part = spread(plain, first)
    row_part = row_part.reshape(n_far, 2, block, -1)
    crossed = over_col(row_part[:, 1], 1)
    chip_part = row_part[:, 0].astype(F32) + crossed.astype(F32)
    chip_part = chip_part.astype(BF16)
    ends = [chip_part[0]] + [over_col(chip_part[j], 2 * j) for j in range(1, n_far)]
    node_grad = last(ends, w_one)

    row_features = jnp.stack([value for pair in zip(near_features, other_features) for value in pair])
    term_one = lax.dot_general(
        row_features.reshape(n_col * block, -1),
        row_part.reshape(n_col * block, -1),
        ROWS_COLS,
        preferred_element_type=F32,
    )
    terms = jnp.stack([term_one, term_two]).astype(BF16)
    half = terms.shape[1] // 2
    odd = col % 2 == 1
    mine = jnp.where(odd, terms[:, half:], terms[:, :half])
    yours = jnp.where(odd, terms[:, :half], terms[:, half:])
    total = (mine.astype(F32) + over_col(yours, 1).astype(F32)).astype(BF16)
    total = tree([value.astype(F32) for value in rows_all(total)]).astype(BF16)
    total = tree([value.astype(F32) for value in far(total)]) * scale
    other = over_col(total, 1)
    total = jnp.concatenate([jnp.where(odd, other, total), jnp.where(odd, total, other)], axis=1)
    return node_grad, total[0], total[1]


def solution(mesh):
    return jax.shard_map(
        functools.partial(local, mesh.shape["row"], mesh.shape["col"]),
        mesh=mesh,
        in_specs=(
            P("row", "col"),
            P("row", "col"),
            P(("row", "col"), None),
            P(("row", "col"), None),
            P(("col", "row"), None),
            P(("col", "row"), None),
            P(("row", "col"), None),
            P(),
            P(),
        ),
        out_specs=(P(("row", "col"), None), P(), P()),
        check_vma=False,
    )
```

```python
import functools

import jax
import jax.numpy as jnp
from jax import lax
from jax.experimental import pallas as pl
from jax.experimental.pallas import tpu as pltpu
from jax.sharding import PartitionSpec as P

BF16, F32 = jnp.bfloat16, jnp.float32
ROWS_COLS = (((0,), (0,)), ((), ()))
LAST_LAST = (((1,), (1,)), ((), ()))
VMEM = pltpu.VMEM


def params():
    return pltpu.CompilerParams(vmem_limit_bytes=16 * 1024 * 1024)


def cost(flops, bytes_accessed):
    return pl.CostEstimate(flops=flops, bytes_accessed=bytes_accessed, transcendentals=0)


def whole(count):
    return [pl.BlockSpec(memory_space=VMEM) for _ in range(count)]


def unread(events):
    return whole(len(events))


def tree(values):
    while len(values) > 1:
        values = [a + b for a, b in zip(values[::2], values[1::2])]
    return values[0]


def mask_kernel(block, tile, row_src, col_src, mask, adj, plain, token):
    step = pl.program_id(0)
    per = block // tile
    row = row_src[step]
    token[...] = jnp.zeros_like(token)
    for slot in range(adj.shape[1] // block):
        col = col_src[slot]
        for v in range(per):
            part = adj[:, pl.ds(pl.multiple_of((col * per + v) * tile, tile), tile)]
            for u in range(per):
                keep = mask[row * per + u, col * per + v].astype(F32).astype(BF16)
                lanes = slice(slot * block + v * tile, slot * block + (v + 1) * tile)
                plain[u * tile : (u + 1) * tile, lanes] = part[u * tile : (u + 1) * tile] * keep


def masked(adjacency, tile_mask, row_src, col_src, block):
    rows, cols = adjacency.shape
    tile = rows // tile_mask.shape[0]
    adjacency = pltpu.with_memory_space_constraint(adjacency, pltpu.HBM)
    return pl.pallas_call(
        functools.partial(mask_kernel, block, tile),
        grid_spec=pltpu.PrefetchScalarGridSpec(
            num_scalar_prefetch=3,
            grid=(rows // block,),
            in_specs=[pl.BlockSpec((block, cols), lambda s, row_src, *_: (row_src[s], 0))],
            out_specs=[
                pl.BlockSpec((block, cols), lambda s, *_: (s, 0)),
                pl.BlockSpec((16, 128), lambda s, *_: (0, 0)),
            ],
        ),
        out_shape=[VMEM((rows, cols), BF16), VMEM((16, 128), BF16)],
        compiler_params=params(),
        cost_estimate=cost(rows * cols, 4 * rows * cols),
        name="mask_tiles",
    )(row_src, col_src, tile_mask, adjacency)


def spread_kernel(count, turned, *refs):
    graph, parts, out, held = refs[0], refs[1 : count + 1], refs[-2], refs[-1]
    block = parts[0].shape[0]
    for slot, part in enumerate(parts):
        held[slot * block : (slot + 1) * block] = part[...]
    chunk = min(out.shape[0], 1024)

    @pl.loop(0, out.shape[0] // chunk)
    def _(step):
        span = pl.ds(pl.multiple_of(step * chunk, chunk), chunk)
        if turned:
            value = lax.dot_general(graph[:, span], held[...], ROWS_COLS, preferred_element_type=F32)
        else:
            value = jnp.dot(graph[span], held[...], preferred_element_type=F32)
        out[span] = value.astype(BF16)


def spread(graph, parts, turned, *events):
    block, width = parts[0].shape
    rows, cols = graph.shape
    out_rows, depth = (cols, rows) if turned else (rows, cols)
    graph = pltpu.with_memory_space_constraint(graph, VMEM)
    out = pl.pallas_call(
        functools.partial(spread_kernel, len(parts), turned),
        in_specs=whole(1 + len(parts)) + unread(events),
        out_specs=pl.BlockSpec(memory_space=VMEM),
        out_shape=jax.ShapeDtypeStruct((out_rows, width), BF16),
        scratch_shapes=[VMEM((depth, width), BF16)],
        compiler_params=params(),
        cost_estimate=cost(2 * rows * cols * width, 2 * rows * cols),
        name="propagate",
    )(graph, *parts, *events)
    return out.reshape(out_rows // block, block, width)


def middle_kernel(count, *refs):
    parts, w_two, pre_one = refs[:count], refs[count], refs[count + 1]
    prop, grad = refs[-2:]
    total = tree([part[...].astype(F32) for part in parts]).astype(BF16)
    prop[...] = total
    back = lax.dot_general(total, w_two[...], LAST_LAST, preferred_element_type=F32)
    grad[...] = jnp.where(pre_one[...] > 0, back, 0.0).astype(BF16)


def middle(parts, w_two, pre_one, *events):
    shape = jax.ShapeDtypeStruct(pre_one.shape, BF16)
    return pl.pallas_call(
        functools.partial(middle_kernel, len(parts)),
        in_specs=whole(len(parts) + 2) + unread(events),
        out_specs=whole(2),
        out_shape=[shape, shape],
        compiler_params=params(),
        name="first_layer_gradient",
    )(*parts, w_two, pre_one, *events)


def last_kernel(count, *refs):
    parts, w_one, out, token = refs[:count], refs[count], refs[-2], refs[-1]
    total = tree([part[...].astype(F32) for part in parts]).astype(BF16)
    out[...] = lax.dot_general(
        total, w_one[...], LAST_LAST, preferred_element_type=F32
    ).astype(BF16)
    token[...] = total[: token.shape[0], : token.shape[1]]


def last(parts, w_one):
    return pl.pallas_call(
        functools.partial(last_kernel, len(parts)),
        in_specs=whole(len(parts) + 1),
        out_specs=whole(2),
        out_shape=[
            jax.ShapeDtypeStruct(parts[0].shape, BF16),
            jax.ShapeDtypeStruct((16, 128), BF16),
        ],
        compiler_params=params(),
        name="node_gradient",
    )(*parts, w_one)


def copy_kernel(value, *refs):
    refs[-1][...] = value[...]


def after(value, *events):
    return pl.pallas_call(
        copy_kernel,
        in_specs=whole(1) + unread(events),
        out_specs=pl.BlockSpec(memory_space=VMEM),
        out_shape=jax.ShapeDtypeStruct(value.shape, value.dtype),
        compiler_params=params(),
        name="after",
    )(value, *events)


def joined_kernel(count, *refs):
    refs[-1][...] = tree([ref[...].astype(F32) for ref in refs[:count]]).astype(BF16)


def joined(values, *events):
    return pl.pallas_call(
        functools.partial(joined_kernel, len(values)),
        in_specs=whole(len(values)) + unread(events),
        out_specs=pl.BlockSpec(memory_space=VMEM),
        out_shape=jax.ShapeDtypeStruct(values[0].shape, BF16),
        compiler_params=params(),
        name="joined",
    )(*values, *events)


def xor_order(blocks, bits):
    for position, bit in enumerate(bits):
        split = blocks.reshape((-1, 2, 1 << position) + blocks.shape[1:])
        blocks = jnp.where(bit, split[:, ::-1], split).reshape(blocks.shape)
    return blocks


def local(n_row, n_col, adjacency, tile_mask, out_grad, pre_two, hidden, pre_one, features, w_two, w_one):
    block = out_grad.shape[0]
    scale = 4.0 * block ** (-0.5)
    n_far = n_col // 2
    row, col = lax.axis_index("row"), lax.axis_index("col")
    odd = col % 2 == 1

    def over_col(value, flip):
        return lax.ppermute(value, "col", [(i, i ^ flip) for i in range(n_col)])

    def over_row(value, flip):
        return lax.ppermute(value, "row", [(i, i ^ flip) for i in range(n_row)])

    def far(values):
        got = {j: over_col(values[j], 2 * j) for j in reversed(range(1, n_far))}
        return [values[0]] + [got[j] for j in range(1, n_far)]

    def rows_all(values):
        got = {i: over_row(values[i], i) for i in reversed(range(1, n_row))}
        return [values[0]] + [got[i] for i in range(1, n_row)]

    def halved(term):
        half = term.shape[0] // 2
        mine = jnp.where(odd, term[half:], term[:half])
        yours = jnp.where(odd, term[:half], term[half:]).astype(BF16)
        return (mine + over_col(yours, 1).astype(F32)).astype(BF16)

    def sum_far(value):
        return tree([v.astype(F32) for v in far([value] * n_far)]).astype(BF16)

    row_src = jnp.bitwise_xor(jnp.arange(n_col, dtype=jnp.int32), col)
    col_src = jnp.bitwise_xor(jnp.arange(n_row, dtype=jnp.int32), row)

    grad_two = jnp.where(pre_two > 0, out_grad, jnp.zeros_like(out_grad))
    near = far([grad_two] * n_far)
    near_features = [features, over_col(features, 2)]
    plain, made = masked(adjacency, tile_mask, row_src, col_src, block)
    others = [over_col(after(value, made), 1) for value in near]
    column_part = spread(plain, [value for pair in zip(near, others) for value in pair], True)
    parts = rows_all(column_part)
    late_features = after(features, *near[1:])
    near_features += [over_col(late_features, 2 * j) for j in range(2, n_far)]
    prop_two, grad_one = middle(parts, w_two, pre_one, near_features[1])
    first = rows_all([grad_one] * n_row)
    other_features = [over_col(value, 1) for value in near_features]
    row_features = jnp.stack([value for pair in zip(near_features, other_features) for value in pair])

    row_part = spread(plain, first, False, row_features)
    row_part = row_part.reshape(n_far, 2, block, -1)
    crossed = over_col(row_part[:, 1], 1)
    chip_part = row_part[:, 0].astype(F32) + crossed.astype(F32)
    chip_part = chip_part.astype(BF16)
    ends = far(chip_part)
    node_grad, token = last(ends, w_one)

    term_two = lax.dot_general(hidden, prop_two, ROWS_COLS, preferred_element_type=F32)
    term_one = lax.dot_general(
        row_features.reshape(n_col * block, -1),
        row_part.reshape(n_col * block, -1),
        ROWS_COLS,
        preferred_element_type=F32,
    )
    width = term_one.shape[1]
    terms = jnp.stack([halved(term_one), halved(term_two)], axis=1)
    terms = terms.reshape(n_row, -1, width)
    row_bits = [jnp.bitwise_and(row, 1 << b) > 0 for b in range(n_row.bit_length() - 1)]
    terms = xor_order(terms, row_bits)
    total = tree([value.astype(F32) for value in rows_all(terms)]).astype(BF16)
    total = joined([total] + [over_col(total, 2 * j) for j in range(1, n_far)], token)
    total = xor_order(jnp.stack(rows_all([total] * n_row)), row_bits)
    total = total.reshape(-1, 2, width).astype(F32) * scale
    other = over_col(total, 1)
    lower, upper = jnp.where(odd, other, total), jnp.where(odd, total, other)
    total = jnp.concatenate([lower, upper], axis=0)
    return node_grad, total[:, 0], total[:, 1]


def solution(mesh):
    return jax.shard_map(
        functools.partial(local, mesh.shape["row"], mesh.shape["col"]),
        mesh=mesh,
        in_specs=(
            P("row", "col"),
            P("row", "col"),
            P(("row", "col"), None),
            P(("row", "col"), None),
            P(("col", "row"), None),
            P(("col", "row"), None),
            P(("row", "col"), None),
            P(),
            P(),
        ),
        out_specs=(P(("row", "col"), None), P(), P()),
        check_vma=False,
    )
```

```python
import functools

import jax
import jax.numpy as jnp
from jax import lax
from jax.experimental import pallas as pl
from jax.experimental.pallas import tpu as pltpu
from jax.sharding import PartitionSpec as P

BF16, F32 = jnp.bfloat16, jnp.float32
ROWS_COLS = (((0,), (0,)), ((), ()))
LAST_LAST = (((1,), (1,)), ((), ()))
VMEM = pltpu.VMEM


def params():
    return pltpu.CompilerParams(vmem_limit_bytes=16 * 1024 * 1024)


def cost(flops, bytes_accessed):
    return pl.CostEstimate(flops=flops, bytes_accessed=bytes_accessed, transcendentals=0)


def whole(count):
    return [pl.BlockSpec(memory_space=VMEM) for _ in range(count)]


def unread(events):
    return whole(len(events))


def tree(values):
    while len(values) > 1:
        values = [a + b for a, b in zip(values[::2], values[1::2])]
    return values[0]


def mask_kernel(block, tile, row_src, col_src, mask, adj, plain, token):
    step = pl.program_id(0)
    per = block // tile
    row = row_src[step]
    token[...] = jnp.zeros_like(token)
    for slot in range(adj.shape[1] // block):
        col = col_src[slot]
        for v in range(per):
            part = adj[:, pl.ds(pl.multiple_of((col * per + v) * tile, tile), tile)]
            for u in range(per):
                keep = mask[row * per + u, col * per + v].astype(F32).astype(BF16)
                lanes = slice(slot * block + v * tile, slot * block + (v + 1) * tile)
                plain[u * tile : (u + 1) * tile, lanes] = part[u * tile : (u + 1) * tile] * keep


def masked(adjacency, tile_mask, row_src, col_src, block):
    rows, cols = adjacency.shape
    tile = rows // tile_mask.shape[0]
    adjacency = pltpu.with_memory_space_constraint(adjacency, pltpu.HBM)
    return pl.pallas_call(
        functools.partial(mask_kernel, block, tile),
        grid_spec=pltpu.PrefetchScalarGridSpec(
            num_scalar_prefetch=3,
            grid=(rows // block,),
            in_specs=[pl.BlockSpec((block, cols), lambda s, row_src, *_: (row_src[s], 0))],
            out_specs=[
                pl.BlockSpec((block, cols), lambda s, *_: (s, 0)),
                pl.BlockSpec((16, 128), lambda s, *_: (0, 0)),
            ],
        ),
        out_shape=[VMEM((rows, cols), BF16), VMEM((16, 128), BF16)],
        compiler_params=params(),
        cost_estimate=cost(rows * cols, 4 * rows * cols),
        name="mask_tiles",
    )(row_src, col_src, tile_mask, adjacency)


def spread_kernel(count, turned, *refs):
    graph, parts, out, held = refs[0], refs[1 : count + 1], refs[-2], refs[-1]
    block = parts[0].shape[0]
    for slot, part in enumerate(parts):
        held[slot * block : (slot + 1) * block] = part[...]
    chunk = min(out.shape[0], 1024)

    @pl.loop(0, out.shape[0] // chunk)
    def _(step):
        span = pl.ds(pl.multiple_of(step * chunk, chunk), chunk)
        if turned:
            value = lax.dot_general(graph[:, span], held[...], ROWS_COLS, preferred_element_type=F32)
        else:
            value = jnp.dot(graph[span], held[...], preferred_element_type=F32)
        out[span] = value.astype(BF16)


def spread(graph, parts, turned, *events):
    block, width = parts[0].shape
    rows, cols = graph.shape
    out_rows, depth = (cols, rows) if turned else (rows, cols)
    graph = pltpu.with_memory_space_constraint(graph, VMEM)
    out = pl.pallas_call(
        functools.partial(spread_kernel, len(parts), turned),
        in_specs=whole(1 + len(parts)) + unread(events),
        out_specs=pl.BlockSpec(memory_space=VMEM),
        out_shape=jax.ShapeDtypeStruct((out_rows, width), BF16),
        scratch_shapes=[VMEM((depth, width), BF16)],
        compiler_params=params(),
        cost_estimate=cost(2 * rows * cols * width, 2 * rows * cols),
        name="propagate",
    )(graph, *parts, *events)
    return out.reshape(out_rows // block, block, width)


def middle_kernel(count, *refs):
    parts, w_two, pre_one = refs[:count], refs[count], refs[count + 1]
    prop, grad = refs[-2:]
    total = tree([part[...].astype(F32) for part in parts]).astype(BF16)
    prop[...] = total
    back = lax.dot_general(total, w_two[...], LAST_LAST, preferred_element_type=F32)
    grad[...] = jnp.where(pre_one[...] > 0, back, 0.0).astype(BF16)


def middle(parts, w_two, pre_one, *events):
    shape = jax.ShapeDtypeStruct(pre_one.shape, BF16)
    return pl.pallas_call(
        functools.partial(middle_kernel, len(parts)),
        in_specs=whole(len(parts) + 2) + unread(events),
        out_specs=whole(2),
        out_shape=[shape, shape],
        compiler_params=params(),
        name="first_layer_gradient",
    )(*parts, w_two, pre_one, *events)


def last_kernel(total, w_one, out):
    out[...] = lax.dot_general(
        total[...], w_one[...], LAST_LAST, preferred_element_type=F32
    ).astype(BF16)


def last(total, w_one):
    return pl.pallas_call(
        last_kernel,
        in_specs=whole(2),
        out_specs=pl.BlockSpec(memory_space=VMEM),
        out_shape=jax.ShapeDtypeStruct(total.shape, BF16),
        compiler_params=params(),
        name="node_gradient",
    )(total, w_one)


def copy_kernel(value, *refs):
    refs[-1][...] = value[...]


def after(value, *events):
    return pl.pallas_call(
        copy_kernel,
        in_specs=whole(1) + unread(events),
        out_specs=pl.BlockSpec(memory_space=VMEM),
        out_shape=jax.ShapeDtypeStruct(value.shape, value.dtype),
        compiler_params=params(),
        name="after",
    )(value, *events)


def joined_kernel(count, *refs):
    out = refs[-1]
    out[...] = tree([ref[...].astype(F32) for ref in refs[:count]]).astype(out.dtype)


def joined(values, *events, dtype=BF16):
    return pl.pallas_call(
        functools.partial(joined_kernel, len(values)),
        in_specs=whole(len(values)) + unread(events),
        out_specs=pl.BlockSpec(memory_space=VMEM),
        out_shape=jax.ShapeDtypeStruct(values[0].shape, dtype),
        compiler_params=params(),
        name="joined",
    )(*values, *events)


def scaled_kernel(scale, odd, mine, other, *outs):
    half = mine.shape[1]
    for i, out in enumerate(outs):
        out[pl.ds(pl.multiple_of(odd[0] * half, half), half)] = mine[i] * scale
        out[pl.ds(pl.multiple_of((1 - odd[0]) * half, half), half)] = other[i] * scale


def scaled(odd, mine, other, scale):
    count, half, width = mine.shape
    return pl.pallas_call(
        functools.partial(scaled_kernel, scale),
        in_specs=[pl.BlockSpec(memory_space=pltpu.SMEM)] + whole(2),
        out_specs=whole(count),
        out_shape=[jax.ShapeDtypeStruct((2 * half, width), F32)] * count,
        compiler_params=params(),
        name="weight_gradients",
    )(odd, mine, other)


def local(n_row, n_col, adjacency, tile_mask, out_grad, pre_two, hidden, pre_one, features, w_two, w_one):
    block = out_grad.shape[0]
    scale = 4.0 * block ** (-0.5)
    n_far = n_col // 2
    row, col = lax.axis_index("row"), lax.axis_index("col")
    odd = col % 2 == 1

    def over_col(value, flip):
        return lax.ppermute(value, "col", [(i, i ^ flip) for i in range(n_col)])

    def over_row(value, flip):
        return lax.ppermute(value, "row", [(i, i ^ flip) for i in range(n_row)])

    def far(values):
        got = {j: over_col(values[j], 2 * j) for j in reversed(range(1, n_far))}
        return [values[0]] + [got[j] for j in range(1, n_far)]

    def rows_all(values):
        got = {i: over_row(values[i], i) for i in reversed(range(1, n_row))}
        return [values[0]] + [got[i] for i in range(1, n_row)]

    def halved(term):
        half = term.shape[0] // 2
        mine = jnp.where(odd, term[half:], term[:half])
        yours = jnp.where(odd, term[:half], term[half:]).astype(BF16)
        return (mine + over_col(yours, 1).astype(F32)).astype(BF16)

    def sum_far(value):
        return tree([v.astype(F32) for v in far([value] * n_far)]).astype(BF16)

    row_src = jnp.bitwise_xor(jnp.arange(n_col, dtype=jnp.int32), col)
    col_src = jnp.bitwise_xor(jnp.arange(n_row, dtype=jnp.int32), row)

    grad_two = jnp.where(pre_two > 0, out_grad, jnp.zeros_like(out_grad))
    near = far([grad_two] * n_far)
    near_features = [features, over_col(features, 2)]
    plain, made = masked(adjacency, tile_mask, row_src, col_src, block)
    others = [over_col(after(value, made), 1) for value in near]
    column_part = spread(plain, [value for pair in zip(near, others) for value in pair], True)
    parts = rows_all(column_part)
    late_features = after(features, *near[1:])
    near_features += [over_col(late_features, 2 * j) for j in range(2, n_far)]
    prop_two, grad_one = middle(parts, w_two, pre_one, near_features[1])
    first = rows_all([grad_one] * n_row)
    other_features = [over_col(value, 1) for value in near_features]
    row_features = jnp.stack([value for pair in zip(near_features, other_features) for value in pair])

    row_part = spread(plain, first, False, row_features)
    row_part = row_part.reshape(n_far, 2, block, -1)
    crossed = over_col(row_part[:, 1], 1)
    chip_part = row_part[:, 0].astype(F32) + crossed.astype(F32)
    chip_part = chip_part.astype(BF16)
    ends = far(chip_part)
    prop_one = joined(ends)
    node_grad = last(prop_one, w_one)

    term_two = lax.dot_general(hidden, prop_two, ROWS_COLS, preferred_element_type=F32)
    term_one = lax.dot_general(
        row_features.reshape(n_col * block, -1),
        row_part.reshape(n_col * block, -1),
        ROWS_COLS,
        preferred_element_type=F32,
    )
    low, high = range(1, n_col.bit_length() - 2), n_col.bit_length() - 2
    ahead = halved(term_two)
    ahead = joined([ahead, over_col(ahead, 1 << high)])
    total = joined(rows_all([jnp.stack([halved(term_one), ahead])] * n_row))
    for bit in low:
        total = joined([total, over_col(total, 1 << bit)], prop_one)
    one = joined([total[0], over_col(total[0], 1 << high)], dtype=F32)
    total = jnp.stack([one, total[1].astype(F32)])
    odd = jnp.bitwise_and(col, 1).reshape(1)
    return node_grad, *scaled(odd, total, over_col(total, 1), scale)


def solution(mesh):
    return jax.shard_map(
        functools.partial(local, mesh.shape["row"], mesh.shape["col"]),
        mesh=mesh,
        in_specs=(
            P("row", "col"),
            P("row", "col"),
            P(("row", "col"), None),
            P(("row", "col"), None),
            P(("col", "row"), None),
            P(("col", "row"), None),
            P(("row", "col"), None),
            P(),
            P(),
        ),
        out_specs=(P(("row", "col"), None), P(), P()),
        check_vma=False,
    )
```

```python
import functools

import jax
import jax.numpy as jnp
from jax import lax
from jax.experimental import pallas as pl
from jax.experimental.pallas import tpu as pltpu
from jax.sharding import PartitionSpec as P

BF16, F32 = jnp.bfloat16, jnp.float32
ROWS_COLS = (((0,), (0,)), ((), ()))
LAST_LAST = (((1,), (1,)), ((), ()))
VMEM = pltpu.VMEM


def params():
    return pltpu.CompilerParams(vmem_limit_bytes=16 * 1024 * 1024)


def cost(flops, bytes_accessed):
    return pl.CostEstimate(flops=flops, bytes_accessed=bytes_accessed, transcendentals=0)


def whole(count):
    return [pl.BlockSpec(memory_space=VMEM) for _ in range(count)]


def unread(events):
    return whole(len(events))


def tree(values):
    while len(values) > 1:
        values = [a + b for a, b in zip(values[::2], values[1::2])]
    return values[0]


def mask_kernel(block, tile, row_src, col_src, mask, adj, plain, token):
    step = pl.program_id(0)
    per = block // tile
    row = row_src[step]
    token[...] = jnp.zeros_like(token)
    for slot in range(adj.shape[1] // block):
        col = col_src[slot]
        for v in range(per):
            part = adj[:, pl.ds(pl.multiple_of((col * per + v) * tile, tile), tile)]
            for u in range(per):
                keep = mask[row * per + u, col * per + v].astype(F32).astype(BF16)
                lanes = slice(slot * block + v * tile, slot * block + (v + 1) * tile)
                plain[u * tile : (u + 1) * tile, lanes] = part[u * tile : (u + 1) * tile] * keep


def masked(adjacency, tile_mask, row_src, col_src, block):
    rows, cols = adjacency.shape
    tile = rows // tile_mask.shape[0]
    adjacency = pltpu.with_memory_space_constraint(adjacency, pltpu.HBM)
    return pl.pallas_call(
        functools.partial(mask_kernel, block, tile),
        grid_spec=pltpu.PrefetchScalarGridSpec(
            num_scalar_prefetch=3,
            grid=(rows // block,),
            in_specs=[pl.BlockSpec((block, cols), lambda s, row_src, *_: (row_src[s], 0))],
            out_specs=[
                pl.BlockSpec((block, cols), lambda s, *_: (s, 0)),
                pl.BlockSpec((16, 128), lambda s, *_: (0, 0)),
            ],
        ),
        out_shape=[VMEM((rows, cols), BF16), VMEM((16, 128), BF16)],
        compiler_params=params(),
        name="mask_tiles",
    )(row_src, col_src, tile_mask, adjacency)


def spread_kernel(count, turned, *refs):
    graph, parts, out, held = refs[0], refs[1 : count + 1], refs[-2], refs[-1]
    block = parts[0].shape[0]
    for slot, part in enumerate(parts):
        held[slot * block : (slot + 1) * block] = part[...]
    chunk = min(out.shape[0], 1024)

    @pl.loop(0, out.shape[0] // chunk)
    def _(step):
        span = pl.ds(pl.multiple_of(step * chunk, chunk), chunk)
        if turned:
            value = lax.dot_general(graph[:, span], held[...], ROWS_COLS, preferred_element_type=F32)
        else:
            value = jnp.dot(graph[span], held[...], preferred_element_type=F32)
        out[span] = value.astype(BF16)


def spread(graph, parts, turned, *events):
    block, width = parts[0].shape
    rows, cols = graph.shape
    out_rows, depth = (cols, rows) if turned else (rows, cols)
    graph = pltpu.with_memory_space_constraint(graph, VMEM)
    out = pl.pallas_call(
        functools.partial(spread_kernel, len(parts), turned),
        in_specs=whole(1 + len(parts)) + unread(events),
        out_specs=pl.BlockSpec(memory_space=VMEM),
        out_shape=jax.ShapeDtypeStruct((out_rows, width), BF16),
        scratch_shapes=[VMEM((depth, width), BF16)],
        compiler_params=params(),
        cost_estimate=(cost(2 * rows * cols * width, 2 * rows * cols)) if turned else (cost(24_000_000_000, 1_000_000)),
        name="propagate",
    )(graph, *parts, *events)
    return out.reshape(out_rows // block, block, width)


def put_halves(term, odd, both, mine, yours):
    half = mine.shape[0]
    both[...] = term
    mine[...] = both[pl.ds(pl.multiple_of(odd * half, half), half)]
    yours[...] = both[pl.ds(pl.multiple_of((1 - odd) * half, half), half)].astype(BF16)


def half_shapes(width, columns):
    return [
        jax.ShapeDtypeStruct((width // 2, columns), F32),
        jax.ShapeDtypeStruct((width // 2, columns), BF16),
    ]


def middle_kernel(count, odd, *refs):
    parts = refs[:count]
    w_two, pre_one, hidden = refs[count : count + 3]
    grad, mine, yours, both = refs[-4:]
    total = tree([part[...].astype(F32) for part in parts]).astype(BF16)
    back = lax.dot_general(total, w_two[...], LAST_LAST, preferred_element_type=F32)
    grad[...] = jnp.where(pre_one[...] > 0, back, 0.0).astype(BF16)
    term = lax.dot_general(hidden[...], total, ROWS_COLS, preferred_element_type=F32)
    put_halves(term, odd[0], both, mine, yours)


def middle(odd, parts, w_two, pre_one, hidden, *events):
    width = hidden.shape[1]
    return pl.pallas_call(
        functools.partial(middle_kernel, len(parts)),
        in_specs=[pl.BlockSpec(memory_space=pltpu.SMEM)] + whole(len(parts) + 3) + unread(events),
        out_specs=whole(3),
        out_shape=[jax.ShapeDtypeStruct(pre_one.shape, BF16)] + half_shapes(width, width),
        scratch_shapes=[VMEM((width, width), F32)],
        compiler_params=params(),
        name="first_layer_gradient",
    )(odd, *parts, w_two, pre_one, hidden, *events)


def last_kernel(total, w_one, out):
    out[...] = lax.dot_general(
        total[...], w_one[...], LAST_LAST, preferred_element_type=F32
    ).astype(BF16)


def last(total, w_one):
    return pl.pallas_call(
        last_kernel,
        in_specs=whole(2),
        out_specs=pl.BlockSpec(memory_space=VMEM),
        out_shape=jax.ShapeDtypeStruct(total.shape, BF16),
        compiler_params=params(),
        name="node_gradient",
    )(total, w_one)


def copy_kernel(value, *refs):
    refs[-1][...] = value[...]


def after(value, *events):
    return pl.pallas_call(
        copy_kernel,
        in_specs=whole(1) + unread(events),
        out_specs=pl.BlockSpec(memory_space=VMEM),
        out_shape=jax.ShapeDtypeStruct(value.shape, value.dtype),
        compiler_params=params(),
        name="after",
    )(value, *events)


def joined_kernel(count, *refs):
    out = refs[-1]
    out[...] = tree([ref[...].astype(F32) for ref in refs[:count]]).astype(out.dtype)


def joined(values, *events, dtype=BF16):
    return pl.pallas_call(
        functools.partial(joined_kernel, len(values)),
        in_specs=whole(len(values)) + unread(events),
        out_specs=pl.BlockSpec(memory_space=VMEM),
        out_shape=jax.ShapeDtypeStruct(values[0].shape, dtype),
        compiler_params=params(),
        name="joined",
    )(*values, *events)


def scaled_kernel(scale, odd, mine, other, *outs):
    half = mine.shape[1]
    for i, out in enumerate(outs):
        out[pl.ds(pl.multiple_of(odd[0] * half, half), half)] = mine[i] * scale
        out[pl.ds(pl.multiple_of((1 - odd[0]) * half, half), half)] = other[i] * scale


def scaled(odd, mine, other, scale):
    count, half, width = mine.shape
    return pl.pallas_call(
        functools.partial(scaled_kernel, scale),
        in_specs=[pl.BlockSpec(memory_space=pltpu.SMEM)] + whole(2),
        out_specs=whole(count),
        out_shape=[jax.ShapeDtypeStruct((2 * half, width), F32)] * count,
        compiler_params=params(),
        name="weight_gradients",
    )(odd, mine, other)


def local(n_row, n_col, adjacency, tile_mask, out_grad, pre_two, hidden, pre_one, features, w_two, w_one):
    block = out_grad.shape[0]
    scale = 4.0 * block ** (-0.5)
    n_far = n_col // 2
    high = n_col.bit_length() - 2
    row, col = lax.axis_index("row"), lax.axis_index("col")
    odd = jnp.bitwise_and(col, 1).reshape(1)

    def over_col(value, flip):
        return lax.ppermute(value, "col", [(i, i ^ flip) for i in range(n_col)])

    def over_row(value, flip):
        return lax.ppermute(value, "row", [(i, i ^ flip) for i in range(n_row)])

    def far(values, back):
        order = range(1, n_far)
        got = {j: over_col(values[j], 2 * j) for j in (reversed(order) if back else order)}
        return [values[0]] + [got[j] for j in range(1, n_far)]

    def rows_all(values, back):
        order = range(1, n_row)
        got = {i: over_row(values[i], i) for i in (reversed(order) if back else order)}
        return [values[0]] + [got[i] for i in range(1, n_row)]

    def halved(mine, yours):
        return joined([mine, over_col(yours, 1)])

    row_src = jnp.bitwise_xor(jnp.arange(n_col, dtype=jnp.int32), col)
    col_src = jnp.bitwise_xor(jnp.arange(n_row, dtype=jnp.int32), row)
    grad_two = jnp.where(pre_two > 0, out_grad, jnp.zeros_like(out_grad))
    near = far([grad_two] * n_far, 1)
    near_features = [features, over_col(features, 2)]
    plain, made = masked(adjacency, tile_mask, row_src, col_src, block)
    others = [over_col(after(value, made), 1) for value in near]
    column_part = spread(plain, [value for pair in zip(near, others) for value in pair], True)
    parts = rows_all(column_part, 1)
    late_features = after(features, column_part)
    late = {j: over_col(late_features, 2 * j) for j in range(2, n_far)}
    near_features += [late[j] for j in range(2, n_far)]
    grad_one, *halves_two = middle(odd, parts, w_two, pre_one, hidden)
    first = rows_all([grad_one] * n_row, 1)
    other_features = [over_col(value, 1) for value in near_features]
    all_features = [value for pair in zip(near_features, other_features) for value in pair]
    two = halved(*halves_two)
    two = joined(far([two] * n_far, 1))
    row_features = jnp.stack(all_features)
    row_part = spread(plain, first, False, row_features).reshape(n_far, 2, block, -1)
    term = lax.dot_general(
        row_features.reshape(n_col * block, -1),
        row_part.reshape(n_col * block, -1),
        ROWS_COLS,
        preferred_element_type=F32,
    )
    half = term.shape[0] // 2
    is_odd = odd[0] == 1
    halves_one = (
        jnp.where(is_odd, term[half:], term[:half]),
        jnp.where(is_odd, term[:half], term[half:]).astype(BF16),
    )
    crossed = over_col(row_part[:, 1], 1)
    held = (row_part[:, 0].astype(F32) + crossed.astype(F32)).astype(BF16)
    one = halved(*halves_one)
    steps = []
    for bit in range(1, high + 1):
        pairs = held.reshape((-1, 2) + held.shape[1:])
        held = joined([pairs[:, 0], over_col(pairs[:, 1], 1 << bit)])
        steps.append(held)
    prop_one, step_one = held[0], steps[0]
    total = joined(rows_all([jnp.stack([one, two])] * n_row, 1), step_one)
    one, two = total[0], total[1].astype(F32)
    for bit in range(1, high):
        one = joined([one, over_col(one, 1 << bit)])
    one = joined([one, over_col(one, 1 << high)], prop_one, dtype=F32)
    node_grad = last(prop_one, w_one)
    one, = scaled(odd, one[None], over_col(one, 1)[None], scale)
    two, = scaled(odd, two[None], over_col(two, 1)[None], scale)
    return node_grad, one, two


def solution(mesh):
    return jax.shard_map(
        functools.partial(local, mesh.shape["row"], mesh.shape["col"]),
        mesh=mesh,
        in_specs=(
            P("row", "col"),
            P("row", "col"),
            P(("row", "col"), None),
            P(("row", "col"), None),
            P(("col", "row"), None),
            P(("col", "row"), None),
            P(("row", "col"), None),
            P(),
            P(),
        ),
        out_specs=(P(("row", "col"), None), P(), P()),
        check_vma=False,
    )
```
